512 devices in a mesh: gx: 16 (over x, z_hi), gy: 32 (over z_lo, y, core).
Axes of the slice: x: 4, y: 8, z: 8 (z_hi: 4, z_lo: 2; z = z_hi * 2 + z_lo), core: 2. Of those that a mesh axis runs over, the one named last changes fastest.
Arguments:
- stem_tensor: float32 [512, 512, 512], P('gx', 'gy'), may hold values from -6 to 6
- branch_pool: float32 [8, 512, 512], P(None, 'gy'), may hold values from -0.25 to 0.25
- path_ids: int32 [4], replicated, may hold values from 0 to 7
- mode_orders: int32 [4, 9], replicated, may hold values from 0 to 8, each once within a row
Outputs:
- contracted: float32 [512, 512, 512], P('gx', 'gy')
The draws below stay inside these ranges and needn't reach their ends.
All inputs are finite; a program needn't handle non-finite values.
Results may differ from the reference program's by a relative error of at most 0.00015.
Values sent between devices are 32-bit elements; how exact they have to be, the bound alone decides.
A program may use at most 64 MiB of HBM per device.

```python
import jax
import jax.numpy as jnp
from jax import lax

QUBITS = 9
STEPS = 4
POOL = 8
W = 512


def set_ends(values, own_key, low, high):
    shape = values.shape
    spot = [jax.random.randint(jax.random.fold_in(own_key, axis), (), 0, shape[axis]) for axis in range(len(shape))]
    values = values.at[tuple(spot)].set(low)
    longest = shape.index(max(shape))
    spot[longest] = (spot[longest] + 1) % shape[longest]
    return values.at[tuple(spot)].set(high)


def level_of(own_key, dims, shards, smallest, high):
    gain = 1.0
    for dim, blocks in shards:
        heights = jax.random.uniform(jax.random.fold_in(jax.random.fold_in(own_key, 6), dim), (blocks,), jnp.float32, smallest / len(shards), high / len(shards))
        gain = gain * jnp.repeat(jnp.exp(heights), dims[dim] // blocks).reshape((-1,) + (1,) * (len(dims) - 1 - dim))
    return gain


def centred(rng, shape, width, most, pieces=(), kind=jnp.bfloat16):
    entries = jax.random.normal(rng, shape, jnp.float32) * width
    if len(pieces) > 0:
        entries = level_of(rng, shape, pieces, -0.22, 0.18) * entries
    return jnp.clip(entries, min=-most, max=most).astype(kind)


def setup_inputs(seed: int = 0) -> dict:
    arg_keys = jax.random.split(jax.random.key(seed), 5)
    stem_tensor = centred(arg_keys[0], (W, W, W), 1.0, 6.0, ((0, 16), (1, 32)), jnp.float32)
    branch_pool = centred(arg_keys[1], (POOL, W, W), W ** -0.5, 0.25, ((1, 32),), jnp.float32)
    path_ids = set_ends(jax.random.randint(arg_keys[2], (STEPS,), 0, POOL), jax.random.fold_in(arg_keys[2], 1), 0, POOL - 1).astype(jnp.int32)
    mode_orders = jax.vmap(lambda own: jax.random.permutation(own, QUBITS))(jax.random.split(arg_keys[3], STEPS)).reshape((STEPS, QUBITS)).astype(jnp.int32)
    return {"stem_tensor": stem_tensor, "branch_pool": branch_pool, "path_ids": path_ids, "mode_orders": mode_orders}


def row_order(mode_orders, step, extent):
    qubits = mode_orders.shape[1]
    index_of_row = jnp.arange(extent, dtype=jnp.int32)
    shift_list = jnp.arange(qubits, dtype=jnp.int32)
    bit_table = jnp.right_shift(index_of_row[:, None], shift_list[None, :]) & 1
    powers = jnp.left_shift(jnp.ones((qubits,), jnp.int32), mode_orders[step])
    return jnp.sum(bit_table * powers[None, :], axis=1).astype(jnp.int32)


def reference(stem_tensor, branch_pool, path_ids, mode_orders):
    extent = branch_pool.shape[2]
    stem_array = stem_tensor
    groups = [2, 1, 0, 2]
    for step in range(STEPS):
        chosen = lax.dynamic_index_in_dim(branch_pool, path_ids[step], 0, keepdims=False)
        branch_matrix = jnp.take(chosen, row_order(mode_orders, step, extent), axis=0)
        group = groups[step]
        stem_array = jnp.tensordot(stem_array, branch_matrix, axes=([group], [0]), precision=lax.Precision.HIGHEST)
        stem_array = jnp.moveaxis(stem_array, -1, group)
    return jnp.transpose(stem_array, (1, 2, 0))
```

```python
import functools

import jax
import jax.numpy as jnp
from jax import lax
from jax.experimental import pallas as pl
from jax.experimental.pallas import tpu as pltpu
from jax.sharding import PartitionSpec as P

MESH = pl.DeviceIdType.MESH
F32 = jnp.float32
BF16 = jnp.bfloat16
W = 512
QUBITS = 9
GX, GY = 16, 32


def halves(x):
    hi = x.astype(BF16)
    return hi, (x - hi.astype(F32)).astype(BF16)


def dot(a, b, dims=((1,), (0,))):
    return lax.dot_general(a, b, (dims, ((), ())), preferred_element_type=F32)


def dot3(a, b):
    return dot(a[0], b[0]) + (dot(a[0], b[1]) + dot(a[1], b[0]))


def swap_blocks(rows):
    lane = lax.broadcasted_iota(jnp.int32, (16, 128), 1)
    rows = list(rows)
    for t in (4, 2, 1):
        low = (lane // (16 * t)) % 2 == 0
        for u in range(8):
            if u & t == 0:
                a, b = rows[u], rows[u + t]
                rows[u] = jnp.where(low, a, pltpu.roll(b, 16 * t, 1))
                rows[u + t] = jnp.where(low, pltpu.roll(a, 128 - 16 * t, 1), b)
    return rows


def kernel(
    stem, pool, path, modes, out,
    sel, bf, xa, b1_hi, b1_lo, b03_hi, b03_lo, b2_hi, b2_lo, tmp, z, s, r,
    pool_sem, own_sem, s_own, r_own, s_y, r_y, s_z, r_z, s_a, r_a, s_f, r_f, s_c, r_c, s_x, r_x, s_o, r_o, all_in,
):
    gx, gy = lax.axis_index("gx"), lax.axis_index("gy")
    x, zh = gx // 4, gx % 4
    zl, y, core = gy // 16, (gy // 2) % 8, gy % 2
    zz = zh * 2 + zl

    def device(x_, y_, z_, core_):
        return {"gx": x_ * 4 + z_ // 2, "gy": (z_ % 2) * 16 + y_ * 2 + core_}

    def send(src, dst, s_sem, r_sem, to):
        pltpu.make_async_remote_copy(
            src_ref=src, dst_ref=dst, send_sem=s_sem, recv_sem=r_sem, device_id=to, device_id_type=MESH
        ).start()

    def wait(ref, sem):
        pltpu.make_async_copy(ref, ref, sem).wait()

    barrier = pltpu.get_barrier_semaphore()
    greeted = [{"gy": (gy + d) % GY} for d in range(1, GY)] + [{"gx": (gx + d) % GX} for d in range(1, GX)]
    for to in greeted:
        pl.semaphore_signal(barrier, inc=1, device_id=to, device_id_type=MESH)
    for h in range(1, 4):
        pl.semaphore_signal(
            barrier, inc=1, device_id={"gx": x * 4 + (zh + h) % 4, "gy": (gy + 16) % GY}, device_id_type=MESH
        )

    own = pltpu.make_async_copy(stem.at[gy], xa.at[pl.ds(0, 16)], own_sem)
    own.start()
    chosen = [
        pltpu.make_async_copy(pool, sel, pool_sem),
    ]
    for c in chosen:
        c.start()
    for c in chosen:
        c.wait()
    lanes_x = pl.ds(pl.multiple_of(x * 128, 128), 128)
    mine = y % 4 == zh
    y_hi = y // 4
    half = pl.multiple_of(core * 256, 256)
    part = pl.multiple_of(half + zz * 32, 32)
    picked = [sel[path[k]] for k in range(4)]
    for k in range(4):
        tmp[pl.ds(16 * k, 16), :] = picked[k]

    pl.semaphore_wait(barrier, (GY - 1) + (GX - 1) + 3)
    for d in range(1, GX):
        pl.semaphore_signal(all_in, inc=1, device_id={"gx": (gx + d) % GX}, device_id_type=MESH)

    own_rows = pl.ds(pl.multiple_of(part + y_hi * 16, 16), 16)

    @pl.when(mine)
    def _():
        for k in range(4):
            bf[k, own_rows, lanes_x] = tmp[pl.ds(16 * k, 16), lanes_x]
        for d in range(1, 8):
            send(bf.at[:, own_rows, lanes_x], bf.at[:, own_rows, lanes_x], s_y, r_y.at[y_hi], device(x, (y + d) % 8, zz, core))

    for d in range(1, GY):
        send(stem.at[(gy + d) % GY], xa.at[pl.ds(16 * d, 16)], s_x, r_x.at[d // 8], {"gy": (gy + d) % GY})

    for yy in range(2):
        @pl.when(jnp.logical_not(jnp.logical_and(mine, y_hi == yy)))
        def _():
            wait(bf.at[:, pl.ds(0, 16), pl.ds(0, 128)], r_y.at[yy])

    order = (0, 3, 1, 2)

    def send_z(k):
        block = bf.at[k, pl.ds(part, 32), lanes_x]
        for d in range(1, 8):
            send(block, block, s_z, r_z.at[k], device(x, y, (zz + d) % 8, core))

    def send_x(k):
        wait(bf.at[k, pl.ds(0, 224), pl.ds(0, 128)], r_z.at[k])
        block = bf.at[k, pl.ds(half, 256), lanes_x]
        for way, d in ((0, 1), (1, 3)):
            send(block, block, s_a, r_a.at[k, way], device((x + d) % 4, y, zz, core))

    def forward_x(k):
        for way, d in ((0, 1), (1, 3)):
            wait(bf.at[k, pl.ds(0, 256), pl.ds(0, 128)], r_a.at[k, way])
            lanes = pl.ds(pl.multiple_of(((x + 4 - d) % 4) * 128, 128), 128)
            block = bf.at[k, pl.ds(pl.multiple_of(half + 128 * way, 128), 128), lanes]
            send(block, block, s_f, r_f.at[k, way], device((x + d) % 4, y, zz, core))

    def send_c(k):
        for way in range(2):
            wait(bf.at[k, pl.ds(0, 128), pl.ds(0, 128)], r_f.at[k, way])
        block = bf.at[k, pl.ds(half, 256)]
        send(block, block, s_c, r_c.at[k], {"gy": gy + 1 - 2 * core})

    def whole(k):
        wait(bf.at[k, pl.ds(0, 256)], r_c.at[k])

    def source_row(k, row):
        q = jnp.zeros_like(row)
        for t in range(QUBITS):
            q = q + ((row >> t) & 1) * (jnp.int32(1) << modes[k, t])
        return q

    at = lax.broadcasted_iota(jnp.int32, (1, W), 1)
    z_at = (at // 32) % 8
    held_row = ((z_at % 2) * 16 + (z_at // 2 + 4 * ((at // 16) % 2)) * 2 + at // 256) * 16 + at % 16

    def permuted(k, row):
        pick = jnp.where(source_row(k, row) == held_row, 1.0, 0.0).astype(BF16)
        hi, lo = halves(bf[k])
        return dot(pick, hi), dot(pick, lo)

    t = lax.broadcasted_iota(jnp.int32, (W, 1), 0)

    for k in order:
        send_z(k)
    send_x(0)
    send_x(3)
    send_x(1)
    forward_x(0)
    forward_x(3)
    send_c(0)
    forward_x(1)
    send_c(3)
    send_x(2)
    whole(0)
    hi, lo = permuted(0, t)
    b1_hi[...] = hi.astype(BF16)
    b1_lo[...] = lo.astype(BF16)
    send_c(1)
    forward_x(2)
    whole(3)
    hi, lo = permuted(3, t)
    turn = (W - 16 * gy) % W
    hi = pltpu.roll(hi, turn, 1).astype(BF16)
    lo = pltpu.roll(lo, turn, 1).astype(BF16)
    b03 = dot3((b1_hi[...], b1_lo[...]), (hi, lo))
    hi, lo = halves(b03)
    b03_hi[...] = hi
    b03_lo[...] = lo

    whole(1)
    hi, lo = permuted(1, ((gy + GY - t // 16) % GY) * 16 + t % 16)
    m_at = (t % 16) * 32 + t // 16
    swap = jnp.where(m_at == at, 1.0, 0.0).astype(BF16)
    b1_hi[...] = dot(swap, hi.astype(BF16), ((1,), (1,))).astype(BF16)
    b1_lo[...] = dot(swap, lo.astype(BF16), ((1,), (1,))).astype(BF16)

    own.wait()
    w = []
    for g in range(4):
        rows = 7 if g == 0 else 8
        wait(xa.at[pl.ds(0, 16 * rows)], r_x.at[g])
        xg = halves(xa[pl.ds(128 * g, 128), :])
        w = halves(dot3(xg, (b03_hi[...], b03_lo[...])))
        if g < 3:
            b1 = (b1_hi[:, pl.ds(128 * g, 128)], b1_lo[:, pl.ds(128 * g, 128)])
            if g == 0:
                z[...] = dot3(b1, w)
            else:
                z[...] += dot3(b1, w)

    pl.semaphore_wait(all_in, GX - 1)
    b1 = (b1_hi[:, pl.ds(384, 128)], b1_lo[:, pl.ds(384, 128)])
    for j in range(4):
        cols = slice(128 * j, 128 * j + 128)
        zj = z[:, cols] + dot3(b1, (w[0][:, cols], w[1][:, cols]))
        for m in range(4):
            turned = swap_blocks([zj[16 * (8 * m + u):16 * (8 * m + u) + 16] for u in range(8)])
            for v in range(8):
                s[pl.ds(128 * j + 16 * v, 16), pl.ds(128 * m, 128)] = turned[v]

        def row_group(jj, first, j=j):
            jrel = 8 * j + jj
            to_y = (gy + jrel) % GY
            for irel in range(first, GX):
                to_x = (gx + irel) % GX
                send(s.at[pl.ds(jrel * 16 + to_x, 1)], r.at[pl.ds(jrel * 16 + irel, 1)], s_o, r_o.at[j], {"gx": to_x, "gy": to_y})

        if j == 0:
            pltpu.make_async_copy(s.at[pl.ds(gx, 1)], r.at[pl.ds(0, 1)], r_o.at[0]).start()
            row_group(0, 1)

        def body(jj, carry, row_group=row_group):
            row_group(jj, 0)
            return carry

        lax.fori_loop(1 if j == 0 else 0, 8, body, 0)

    send_c(2)
    whole(2)
    hi, lo = permuted(2, ((gx + GX - t % 16) % GX) * 32 + (gy + GY - t // 16) % GY)
    b2_hi[...] = hi.astype(BF16)
    b2_lo[...] = lo.astype(BF16)

    for j in range(4):
        wait(r.at[pl.ds(0, 128)], r_o.at[j])
        rows = pl.ds(128 * j, 128)
        rj = halves(jnp.transpose(r[rows, :]))
        term = dot3(rj, (b2_hi[rows, :], b2_lo[rows, :]))
        if j == 0:
            out[...] = term
        else:
            out[...] += term

    @pl.when(mine)
    def _():
        wait(bf.at[:, pl.ds(0, 112), pl.ds(0, 128)], s_y)
    wait(bf.at[:, pl.ds(0, 224), pl.ds(0, 128)], s_z)
    wait(bf.at[0], s_a)
    wait(bf.at[0, pl.ds(0, 256)], s_f)
    wait(bf.at[pl.ds(0, 2)], s_c)
    wait(xa.at[pl.ds(0, 496)], s_x)
    wait(r.at[pl.ds(0, 504)], s_o)
    for e in range(7):
        wait(r.at[pl.ds(e, 1)], s_o)


def on_device(stem, pool, path, modes):
    any_space = pl.BlockSpec(memory_space=pl.ANY)
    smem = pl.BlockSpec(memory_space=pltpu.SMEM)
    square = pltpu.VMEM((W, W), F32)
    piece = pltpu.VMEM((W, W), BF16)
    dma = pltpu.SemaphoreType.DMA
    result = pl.pallas_call(
        kernel,
        out_shape=jax.ShapeDtypeStruct((W, W), F32),
        in_specs=[any_space, any_space, smem, smem],
        out_specs=pl.BlockSpec(memory_space=pltpu.VMEM),
        scratch_shapes=[
            pltpu.VMEM((8, 16, W), F32), pltpu.VMEM((4, W, W), F32), square,
            piece, piece, piece, piece, piece, piece,
            pltpu.VMEM((64, W), F32), square, square, square,
            dma, dma, dma, dma,
            dma, dma((2,)), dma, dma((4,)), dma, dma((4, 2)), dma, dma((4, 2)), dma, dma((4,)),
            dma, dma((4,)), dma, dma((4,)), pltpu.SemaphoreType.REGULAR,
        ],
        compiler_params=pltpu.CompilerParams(collective_id=0, has_side_effects=True, vmem_limit_bytes=48 << 20),
    )(stem, pool, path, modes)
    return result.reshape(32, 16, W)


def solution(mesh):
    return jax.shard_map(
        on_device,
        mesh=mesh,
        in_specs=(P("gx", "gy", None), P(None, "gy", None), P(), P()),
        out_specs=P("gx", "gy", None),
        check_vma=False,
    )
```

```python
import functools

import jax
import jax.numpy as jnp
from jax import lax
from jax.experimental import pallas as pl
from jax.experimental.pallas import tpu as pltpu
from jax.sharding import PartitionSpec as P

MESH = pl.DeviceIdType.MESH
F32 = jnp.float32
BF16 = jnp.bfloat16
W = 512
VMEM = 62 << 20
QUBITS = 9
GX, GY = 16, 32
FIRST = ((0,), (0,))
PACE = (8, 0, 8, 8, 8)


def halves(x):
    hi = x.astype(BF16)
    return hi, (x - hi.astype(F32)).astype(BF16)


def dot(a, b, dims=((1,), (0,))):
    return lax.dot_general(a, b, (dims, ((), ())), preferred_element_type=F32)


def dot3(a, b, dims=((1,), (0,))):
    return dot(a[0], b[0], dims) + (dot(a[0], b[1], dims) + dot(a[1], b[0], dims))


def swap_blocks(rows):
    lane = lax.broadcasted_iota(jnp.int32, (16, 128), 1)
    rows = list(rows)
    for t in (4, 2, 1):
        low = (lane // (16 * t)) % 2 == 0
        for u in range(8):
            if u & t == 0:
                a, b = rows[u], rows[u + t]
                rows[u] = jnp.where(low, a, pltpu.roll(b, 16 * t, 1))
                rows[u + t] = jnp.where(low, pltpu.roll(a, 128 - 16 * t, 1), b)
    return rows


def kernel(
    stem, pool, path_in, modes_in, out,
    path, modes, sel, bf, xa, pick, p_hi, p_lo, q_hi, q_lo, z, s, r,
    in_sem, own_sem, s_y, r_y, s_z, r_z, s_a, r_a, s_f, r_f, s_c, r_c, s_x, r_x, s_o, r_o, all_in,
):
    gx, gy = lax.axis_index("gx"), lax.axis_index("gy")
    x, zh = gx // 4, gx % 4
    zl, y, core = gy // 16, (gy // 2) % 8, gy % 2
    zz = zh * 2 + zl

    def device(x_, y_, z_, core_):
        return {"gx": x_ * 4 + z_ // 2, "gy": (z_ % 2) * 16 + y_ * 2 + core_}

    def send(src, dst, s_sem, r_sem, to):
        pltpu.make_async_remote_copy(
            src_ref=src, dst_ref=dst, send_sem=s_sem, recv_sem=r_sem, device_id=to, device_id_type=MESH
        ).start()

    def wait(ref, sem):
        pltpu.make_async_copy(ref, ref, sem).wait()

    barrier = pltpu.get_barrier_semaphore()
    greeted = [{"gy": (gy + d) % GY} for d in range(1, GY)] + [{"gx": (gx + d) % GX} for d in range(1, GX)]
    greeted += [{"gx": x * 4 + (zh + h) % 4, "gy": (gy + 16) % GY} for h in range(1, 4)]
    for to in greeted:
        pl.semaphore_signal(barrier, inc=1, device_id=to, device_id_type=MESH)

    own = pltpu.make_async_copy(stem.at[gy], xa.at[pl.ds(0, 16)], own_sem)
    taken = [
        pltpu.make_async_copy(pool, sel, in_sem.at[0]),
        pltpu.make_async_copy(path_in, path, in_sem.at[1]),
        pltpu.make_async_copy(modes_in, modes, in_sem.at[2]),
    ]
    for c in taken:
        c.start()
    own.start()
    for c in taken:
        c.wait()

    lanes_x = pl.ds(pl.multiple_of(x * 128, 128), 128)
    mine = y % 4 == zh
    y_hi = y // 4
    half = pl.multiple_of(core * 256, 256)
    part = pl.multiple_of(half + zz * 32, 32)
    own_rows = pl.ds(pl.multiple_of(part + y_hi * 16, 16), 16)

    @pl.when(mine)
    def _():
        for k in range(4):
            bf[k, own_rows, lanes_x] = sel[path[k], :, lanes_x]

    pl.semaphore_wait(barrier, len(greeted))

    @pl.when(mine)
    def _():
        for d in range(1, 8):
            send(bf.at[:, own_rows, lanes_x], bf.at[:, own_rows, lanes_x], s_y, r_y.at[y_hi], device(x, (y + d) % 8, zz, core))

    left = list(range(1, GY))
    pace = list(PACE)

    def some_stem(count=0):
        for _ in range(count or (pace.pop(0) if pace else 0)):
            if left:
                d = left.pop(0)
                send(stem.at[(gy + d) % GY], xa.at[pl.ds(16 * d, 16)], s_x, r_x, {"gy": (gy + d) % GY})

    some_stem()
    for d in range(1, GX):
        pl.semaphore_signal(all_in, inc=1, device_id={"gx": (gx + d) % GX}, device_id_type=MESH)

    t = lax.broadcasted_iota(jnp.int32, (W, 1), 0)
    at = lax.broadcasted_iota(jnp.int32, (1, W), 1)
    z_at = (at // 32) % 8
    held_row = ((z_at % 2) * 16 + (z_at // 2 + 4 * ((at // 16) % 2)) * 2 + at // 256) * 16 + at % 16

    def make_pick(k, row):
        q = jnp.zeros_like(row)
        for b in range(QUBITS):
            q = q + ((row >> b) & 1) * (jnp.int32(1) << modes[k, b])
        pick[k] = jnp.where(q == held_row, 1.0, 0.0).astype(BF16)

    make_pick(0, t)
    make_pick(3, t)

    for yy in range(2):
        @pl.when(jnp.logical_not(jnp.logical_and(mine, y_hi == yy)))
        def _():
            wait(bf.at[:, pl.ds(0, 16), pl.ds(0, 128)], r_y.at[yy])

    def send_z(k):
        block = bf.at[k, pl.ds(part, 32), lanes_x]
        for d in (1, 7, 2, 6, 3, 5, 4):
            send(block, block, s_z, r_z.at[k], device(x, y, (zz + d) % 8, core))

    def send_x(k):
        wait(bf.at[k, pl.ds(0, 224), pl.ds(0, 128)], r_z.at[k])
        block = bf.at[k, pl.ds(half, 256), lanes_x]
        for way, d in ((0, 1), (1, 3)):
            send(block, block, s_a, r_a.at[k, way], device((x + d) % 4, y, zz, core))

    def forward_x(k):
        for way, d in ((0, 1), (1, 3)):
            wait(bf.at[k, pl.ds(0, 256), pl.ds(0, 128)], r_a.at[k, way])
            lanes = pl.ds(pl.multiple_of(((x + 4 - d) % 4) * 128, 128), 128)
            block = bf.at[k, pl.ds(pl.multiple_of(half + 128 * way, 128), 128), lanes]
            send(block, block, s_f, r_f.at[k, way], device((x + d) % 4, y, zz, core))

    def send_c(k):
        for way in range(2):
            wait(bf.at[k, pl.ds(0, 128), pl.ds(0, 128)], r_f.at[k, way])
        block = bf.at[k, pl.ds(half, 256)]
        send(block, block, s_c, r_c.at[k], {"gy": gy + 1 - 2 * core})

    def whole(k):
        wait(bf.at[k, pl.ds(0, 256)], r_c.at[k])
        return halves(bf[k])

    for k in (0, 3, 1):
        send_z(k)
    some_stem()
    make_pick(1, ((gy + GY - t // 16) % GY) * 16 + t % 16)
    make_pick(2, ((gx + GX - t % 16) % GX) * 32 + ((gy // 8 + 4 - t // 128) % 4) * 8 + (t // 16) % 8)
    for k in (0, 3, 1):
        send_x(k)
        some_stem()
    send_z(2)
    forward_x(0)
    some_stem()
    forward_x(3)
    some_stem()
    send_c(0)
    forward_x(1)
    some_stem(GY)
    send_x(2)
    send_c(3)

    hi, lo = whole(0)
    hi, lo = dot(pick[0], hi).astype(BF16), dot(pick[0], lo).astype(BF16)
    p_hi[...] = dot(hi, pick[3]).astype(BF16)
    p_lo[...] = dot(lo, pick[3]).astype(BF16)
    send_c(1)

    b03 = dot3((p_hi[...], p_lo[...]), whole(3))
    p_hi[...], p_lo[...] = halves(b03)

    own.wait()
    wait(xa.at[pl.ds(0, 496)], r_x)
    hi, lo = halves(dot3(halves(xa[...]), (p_hi[...], p_lo[...])))
    q_hi[...] = dot(pick[1], hi, FIRST).astype(BF16)
    q_lo[...] = dot(pick[1], lo, FIRST).astype(BF16)

    forward_x(2)
    p_hi[...], p_lo[...] = whole(1)
    pl.semaphore_wait(all_in, GX - 1)
    for c in range(4):
        to_high = (gy // 8 + c) % 4
        cols = pl.ds(pl.multiple_of(to_high * 128, 128), 128)
        z[...] = dot3((p_hi[...], p_lo[...]), (q_hi[:, cols], q_lo[:, cols]), FIRST)
        for m in range(4):
            turned = swap_blocks([z[pl.ds(8 * m + u, 16, stride=32), :] for u in range(8)])
            for v in range(8):
                s[pl.ds(128 * c + 16 * v, 16), pl.ds(128 * m, 128)] = turned[v]

        def row_group(jj, first, c=c, to_high=to_high):
            low = (gy + jj) % 8
            src = 128 * c + low * 16
            dst = 128 * c + (gy % 8) * 16
            for i in range(first, GX):
                to_x = (gx + i) % GX
                send(s.at[pl.ds(src + to_x, 1)], r.at[pl.ds(dst + i, 1)], s_o, r_o.at[c], {"gx": to_x, "gy": to_high * 8 + low})

        if c == 0:
            own_row = (gy % 8) * 16
            pltpu.make_async_copy(s.at[pl.ds(own_row + gx, 1)], r.at[pl.ds(own_row, 1)], r_o.at[0]).start()
            row_group(0, 1)

        def body(jj, carry, row_group=row_group):
            row_group(jj, 0)
            return carry

        lax.fori_loop(1 if c == 0 else 0, 8, body, 0)

    send_c(2)
    hi, lo = whole(2)
    q_hi[...] = dot(pick[2], hi).astype(BF16)
    q_lo[...] = dot(pick[2], lo).astype(BF16)

    for c in range(4):
        wait(r.at[pl.ds(0, 128)], r_o.at[c])
        rows = pl.ds(128 * c, 128)
        term = dot3(halves(r[rows, :]), (q_hi[rows, :], q_lo[rows, :]), FIRST)
        if c == 0:
            out[...] = term
        else:
            out[...] += term

    @pl.when(mine)
    def _():
        wait(bf.at[:, pl.ds(0, 112), pl.ds(0, 128)], s_y)
    wait(bf.at[:, pl.ds(0, 224), pl.ds(0, 128)], s_z)
    wait(bf.at[0], s_a)
    wait(bf.at[0, pl.ds(0, 256)], s_f)
    wait(bf.at[pl.ds(0, 2)], s_c)
    wait(xa.at[pl.ds(0, 496)], s_x)
    wait(r.at[pl.ds(0, 504)], s_o)
    for e in range(7):
        wait(r.at[pl.ds(e, 1)], s_o)


def on_device(stem, pool, path, modes):
    hbm = pl.BlockSpec(memory_space=pltpu.HBM)
    square = pltpu.VMEM((W, W), F32)
    piece = pltpu.VMEM((W, W), BF16)
    dma = pltpu.SemaphoreType.DMA
    result = pl.pallas_call(
        kernel,
        out_shape=jax.ShapeDtypeStruct((W, W), F32),
        in_specs=[hbm, hbm, hbm, hbm],
        out_specs=pl.BlockSpec(memory_space=pltpu.VMEM),
        scratch_shapes=[
            pltpu.SMEM((4,), jnp.int32), pltpu.SMEM((4, QUBITS), jnp.int32),
            pltpu.VMEM((8, 16, W), F32), pltpu.VMEM((4, W, W), F32), square,
            pltpu.VMEM((4, W, W), BF16), piece, piece, piece, piece,
            pltpu.VMEM((W, 128), F32), square, square,
            dma((3,)), dma,
            dma, dma((2,)), dma, dma((4,)), dma, dma((4, 2)), dma, dma((4, 2)), dma, dma((4,)),
            dma, dma, dma, dma((4,)), pltpu.SemaphoreType.REGULAR,
        ],
        compiler_params=pltpu.CompilerParams(collective_id=0, has_side_effects=True, vmem_limit_bytes=VMEM),
    )(stem, pool, path, modes)
    return result.reshape(32, 16, W)


def solution(mesh):
    return jax.shard_map(
        on_device,
        mesh=mesh,
        in_specs=(P("gx", "gy", None), P(None, "gy", None), P(), P()),
        out_specs=P("gx", "gy", None),
        check_vma=False,
    )
```

```python
import functools

import jax
import jax.numpy as jnp
from jax import lax
from jax.experimental import pallas as pl
from jax.experimental.pallas import tpu as pltpu
from jax.sharding import PartitionSpec as P

MESH = pl.DeviceIdType.MESH
F32 = jnp.float32
BF16 = jnp.bfloat16
W = 512
VMEM = 62 << 20
QUBITS = 9
GX, GY = 16, 32
FIRST = ((0,), (0,))
PACE = (16, 0, 6, 6, 3)


def halves(x):
    hi = x.astype(BF16)
    return hi, (x - hi.astype(F32)).astype(BF16)


def dot(a, b, dims=((1,), (0,))):
    return lax.dot_general(a, b, (dims, ((), ())), preferred_element_type=F32)


def dot3(a, b, dims=((1,), (0,))):
    return dot(a[0], b[0], dims) + (dot(a[0], b[1], dims) + dot(a[1], b[0], dims))


def swap_blocks(rows):
    lane = lax.broadcasted_iota(jnp.int32, (16, 128), 1)
    rows = list(rows)
    for t in (4, 2, 1):
        low = (lane // (16 * t)) % 2 == 0
        for u in range(8):
            if u & t == 0:
                a, b = rows[u], rows[u + t]
                rows[u] = jnp.where(low, a, pltpu.roll(b, 16 * t, 1))
                rows[u + t] = jnp.where(low, pltpu.roll(a, 128 - 16 * t, 1), b)
    return rows


def kernel(
    stem, pool, path_in, modes_in, out,
    path, modes, sel, bf, xa, pick, p_hi, p_lo, q_hi, q_lo, z, s, r,
    in_sem, own_sem, s_y, r_y, s_z, r_z, s_a, r_a, s_f, r_f, s_c, r_c, s_x, r_x, s_o, r_o, all_in,
):
    gx, gy = lax.axis_index("gx"), lax.axis_index("gy")
    x, zh = gx // 4, gx % 4
    zl, y, core = gy // 16, (gy // 2) % 8, gy % 2
    zz = zh * 2 + zl

    def device(x_, y_, z_, core_):
        return {"gx": x_ * 4 + z_ // 2, "gy": (z_ % 2) * 16 + y_ * 2 + core_}

    def send(src, dst, s_sem, r_sem, to):
        pltpu.make_async_remote_copy(
            src_ref=src, dst_ref=dst, send_sem=s_sem, recv_sem=r_sem, device_id=to, device_id_type=MESH
        ).start()

    def wait(ref, sem):
        pltpu.make_async_copy(ref, ref, sem).wait()

    barrier = pltpu.get_barrier_semaphore()
    greeted = [{"gy": (gy + d) % GY} for d in range(1, GY)] + [{"gx": (gx + d) % GX} for d in range(1, GX)]
    greeted += [{"gx": x * 4 + (zh + h) % 4, "gy": (gy + 16) % GY} for h in range(1, 4)]
    for to in greeted:
        pl.semaphore_signal(barrier, inc=1, device_id=to, device_id_type=MESH)

    own = pltpu.make_async_copy(stem.at[gy], xa.at[pl.ds(0, 16)], own_sem)
    taken = [
        pltpu.make_async_copy(pool, sel, in_sem.at[0]),
        pltpu.make_async_copy(path_in, path, in_sem.at[1]),
        pltpu.make_async_copy(modes_in, modes, in_sem.at[2]),
    ]
    for c in taken:
        c.start()
    own.start()
    for c in taken:
        c.wait()

    lanes_x = pl.ds(pl.multiple_of(x * 128, 128), 128)
    mine = y % 4 == zh
    y_hi = y // 4
    half = pl.multiple_of(core * 256, 256)
    part = pl.multiple_of(half + zz * 32, 32)
    own_rows = pl.ds(pl.multiple_of(part + y_hi * 16, 16), 16)

    @pl.when(mine)
    def _():
        for k in range(4):
            bf[k, own_rows, lanes_x] = sel[path[k], :, lanes_x]

    pl.semaphore_wait(barrier, len(greeted))

    @pl.when(mine)
    def _():
        for d in range(1, 8):
            send(bf.at[:, own_rows, lanes_x], bf.at[:, own_rows, lanes_x], s_y, r_y.at[y_hi], device(x, (y + d) % 8, zz, core))

    left = list(range(1, GY))
    pace = list(PACE)

    def some_stem(count=0):
        for _ in range(count or (pace.pop(0) if pace else 0)):
            if left:
                d = left.pop(0)
                send(stem.at[(gy + d) % GY], xa.at[pl.ds(16 * d, 16)], s_x, r_x, {"gy": (gy + d) % GY})

    some_stem()
    for d in range(1, GX):
        pl.semaphore_signal(all_in, inc=1, device_id={"gx": (gx + d) % GX}, device_id_type=MESH)

    t = lax.broadcasted_iota(jnp.int32, (W, 1), 0)
    at = lax.broadcasted_iota(jnp.int32, (1, W), 1)
    z_at = (at // 32) % 8
    held_row = ((z_at % 2) * 16 + (z_at // 2 + 4 * ((at // 16) % 2)) * 2 + at // 256) * 16 + at % 16

    def make_pick(k, row):
        q = jnp.zeros_like(row)
        for b in range(QUBITS):
            q = q + ((row >> b) & 1) * (jnp.int32(1) << modes[k, b])
        pick[k] = jnp.where(q == held_row, 1.0, 0.0).astype(BF16)

    make_pick(0, t)
    make_pick(3, t)

    for yy in range(2):
        @pl.when(jnp.logical_not(jnp.logical_and(mine, y_hi == yy)))
        def _():
            wait(bf.at[:, pl.ds(0, 16), pl.ds(0, 128)], r_y.at[yy])

    def send_z(k):
        block = bf.at[k, pl.ds(part, 32), lanes_x]
        for d in (1, 7, 2, 6, 3, 5, 4):
            send(block, block, s_z, r_z.at[k], device(x, y, (zz + d) % 8, core))

    def send_c(k, d):
        block = bf.at[k, pl.ds(half, 256), pl.ds(pl.multiple_of(((x + d) % 4) * 128, 128), 128)]
        send(block, block, s_c, r_c.at[k], {"gy": gy + 1 - 2 * core})

    def send_x(k):
        wait(bf.at[k, pl.ds(0, 224), pl.ds(0, 128)], r_z.at[k])
        block = bf.at[k, pl.ds(half, 256), lanes_x]
        for way, d in ((0, 1), (1, 3)):
            send(block, block, s_a, r_a.at[k, way], device((x + d) % 4, y, zz, core))
        send_c(k, 0)

    def forward_x(k):
        for way, d in ((0, 1), (1, 3)):
            wait(bf.at[k, pl.ds(0, 256), pl.ds(0, 128)], r_a.at[k, way])
            lanes = pl.ds(pl.multiple_of(((x + 4 - d) % 4) * 128, 128), 128)
            block = bf.at[k, pl.ds(pl.multiple_of(half + 128 * way, 128), 128), lanes]
            send(block, block, s_f, r_f.at[k, way], device((x + d) % 4, y, zz, core))
        for d in (1, 3):
            send_c(k, d)

    def finish_x(k):
        for way in range(2):
            wait(bf.at[k, pl.ds(0, 128), pl.ds(0, 128)], r_f.at[k, way])
        send_c(k, 2)

    def whole(k):
        wait(bf.at[k, pl.ds(0, 256)], r_c.at[k])
        return halves(bf[k])

    for k in (0, 3, 1):
        send_z(k)
    some_stem()
    make_pick(1, ((gy + GY - t // 16) % GY) * 16 + t % 16)
    make_pick(2, ((gx + GX - t % 16) % GX) * 32 + ((gy // 8 + 4 - t // 128) % 4) * 8 + (t // 16) % 8)
    for k in (0, 3, 1):
        send_x(k)
        some_stem()
    send_z(2)
    forward_x(0)
    some_stem()
    forward_x(3)
    some_stem()
    finish_x(0)
    forward_x(1)
    some_stem(GY)
    send_x(2)
    finish_x(3)

    hi, lo = whole(0)
    hi, lo = dot(pick[0], hi).astype(BF16), dot(pick[0], lo).astype(BF16)
    p_hi[...] = dot(hi, pick[3]).astype(BF16)
    p_lo[...] = dot(lo, pick[3]).astype(BF16)
    finish_x(1)

    b03 = dot3((p_hi[...], p_lo[...]), whole(3))
    p_hi[...], p_lo[...] = halves(b03)

    own.wait()
    wait(xa.at[pl.ds(0, 496)], r_x)
    hi, lo = halves(dot3(halves(xa[...]), (p_hi[...], p_lo[...])))
    q_hi[...] = dot(pick[1], hi, FIRST).astype(BF16)
    q_lo[...] = dot(pick[1], lo, FIRST).astype(BF16)

    forward_x(2)
    p_hi[...], p_lo[...] = whole(1)
    pl.semaphore_wait(all_in, GX - 1)
    for c in range(4):
        to_high = (gy // 8 + c) % 4
        cols = pl.ds(pl.multiple_of(to_high * 128, 128), 128)
        z[...] = dot3((p_hi[...], p_lo[...]), (q_hi[:, cols], q_lo[:, cols]), FIRST)
        for m in range(4):
            turned = swap_blocks([z[pl.ds(8 * m + u, 16, stride=32), :] for u in range(8)])
            for v in range(8):
                s[pl.ds(128 * c + 16 * v, 16), pl.ds(128 * m, 128)] = turned[v]

        def row_group(jj, first, c=c, to_high=to_high):
            low = (gy + jj) % 8
            src = 128 * c + low * 16
            dst = 128 * c + (gy % 8) * 16
            for i in range(first, GX):
                to_x = (gx + i) % GX
                send(s.at[pl.ds(src + to_x, 1)], r.at[pl.ds(dst + i, 1)], s_o, r_o.at[c], {"gx": to_x, "gy": to_high * 8 + low})

        if c == 0:
            own_row = (gy % 8) * 16
            pltpu.make_async_copy(s.at[pl.ds(own_row + gx, 1)], r.at[pl.ds(own_row, 1)], r_o.at[0]).start()
            row_group(0, 1)

        def body(jj, carry, row_group=row_group):
            row_group(jj, 0)
            return carry

        lax.fori_loop(1 if c == 0 else 0, 8, body, 0)

    finish_x(2)
    hi, lo = whole(2)
    q_hi[...] = dot(pick[2], hi).astype(BF16)
    q_lo[...] = dot(pick[2], lo).astype(BF16)

    for c in range(4):
        wait(r.at[pl.ds(0, 128)], r_o.at[c])
        rows = pl.ds(128 * c, 128)
        term = dot3(halves(r[rows, :]), (q_hi[rows, :], q_lo[rows, :]), FIRST)
        if c == 0:
            out[...] = term
        else:
            out[...] += term

    @pl.when(mine)
    def _():
        wait(bf.at[:, pl.ds(0, 112), pl.ds(0, 128)], s_y)
    wait(bf.at[:, pl.ds(0, 224), pl.ds(0, 128)], s_z)
    wait(bf.at[0], s_a)
    wait(bf.at[0, pl.ds(0, 256)], s_f)
    wait(bf.at[pl.ds(0, 2)], s_c)
    wait(xa.at[pl.ds(0, 496)], s_x)
    wait(r.at[pl.ds(0, 504)], s_o)
    for e in range(7):
        wait(r.at[pl.ds(e, 1)], s_o)


def on_device(stem, pool, path, modes):
    hbm = pl.BlockSpec(memory_space=pltpu.HBM)
    square = pltpu.VMEM((W, W), F32)
    piece = pltpu.VMEM((W, W), BF16)
    dma = pltpu.SemaphoreType.DMA
    result = pl.pallas_call(
        kernel,
        out_shape=jax.ShapeDtypeStruct((W, W), F32),
        in_specs=[hbm, hbm, hbm, hbm],
        out_specs=pl.BlockSpec(memory_space=pltpu.VMEM),
        scratch_shapes=[
            pltpu.SMEM((4,), jnp.int32), pltpu.SMEM((4, QUBITS), jnp.int32),
            pltpu.VMEM((8, 16, W), F32), pltpu.VMEM((4, W, W), F32), square,
            pltpu.VMEM((4, W, W), BF16), piece, piece, piece, piece,
            pltpu.VMEM((W, 128), F32), square, square,
            dma((3,)), dma,
            dma, dma((2,)), dma, dma((4,)), dma, dma((4, 2)), dma, dma((4, 2)), dma, dma((4,)),
            dma, dma, dma, dma((4,)), pltpu.SemaphoreType.REGULAR,
        ],
        compiler_params=pltpu.CompilerParams(collective_id=0, has_side_effects=True, vmem_limit_bytes=VMEM),
    )(stem, pool, path, modes)
    return result.reshape(32, 16, W)


def solution(mesh):
    return jax.shard_map(
        on_device,
        mesh=mesh,
        in_specs=(P("gx", "gy", None), P(None, "gy", None), P(), P()),
        out_specs=P("gx", "gy", None),
        check_vma=False,
    )
```
